512 devices in a mesh: seq: 64 (over z_lo, x, y), kv: 8 (over z_hi, core).
Axes of the slice: x: 4, y: 8, z: 8 (z_hi: 4, z_lo: 2; z = z_hi * 2 + z_lo), core: 2. Of those that a mesh axis runs over, the one named last changes fastest.
Arguments:
- text_query: bfloat16 [8192, 8192], P('seq', 'kv'), may hold values from -20 to 20, as said below
- vision_key: bfloat16 [2048, 1024], P('seq', 'kv'), may hold values from -4 to 4, as said below
- vision_value: bfloat16 [2048, 1024], P('seq', 'kv'), may hold values from -6 to 6
- grad_output: bfloat16 [8192, 8192], P('seq', 'kv'), may hold values from -192 to 192
- key_weight: bfloat16 [8192, 1024], P('seq', 'kv'), may hold values from -0.1875 to 0.1875
- value_weight: bfloat16 [8192, 1024], P('seq', 'kv'), may hold values from -0.1875 to 0.1875
Outputs:
- grad_query: bfloat16 [8192, 8192], P('seq', 'kv')
- grad_vision: bfloat16 [2048, 8192], P('seq', 'kv')
The draws below stay inside these ranges and needn't reach their ends.
Inputs may be any that keep to these rules, and one draw needn't show every extreme that they name: `text_query`: entries of order one; some rows of single heads may be large multiples of a key row. `vision_key`: entries of order one.
All inputs are finite; a program needn't handle non-finite values.
Results may differ from the reference program's by a relative error of at most 0.02.
Values may be sent and summed in bfloat16 or wider, within the bound.
A program may use at most 64 MiB of HBM per device.

```python
import math
import jax
import jax.numpy as jnp
from jax import lax

HEAD = 128
QPG = 8
VIS_WIDTH = 8192
KV_HEADS = 8
Q_HEADS = 64
TEXT = 8192
VISION = 2048


def structure(key):
    folded = jax.random.fold_in(key, 11)
    key_query, key_keys = jax.random.split(folded, 2)
    queries = jnp.clip(jax.random.normal(key_query, (TEXT, Q_HEADS * HEAD), jnp.float32), -4.0, 4.0)
    keys_all = jnp.clip(jax.random.normal(key_keys, (VISION, KV_HEADS * HEAD), jnp.float32), -4.0, 4.0)
    return (queries, keys_all)


def draw_text_query(key, part):
    return structure(key)[0].astype(jnp.bfloat16)


def draw_vision_key(key, part):
    return structure(key)[1].astype(jnp.bfloat16)


def spiked(entries, own_key, source, target, parts, factor):
    owner, partner = [(jnp.arange(entries.shape[position]) // (entries.shape[position] // parts)).reshape([-1 if axis == position else 1 for axis in range(entries.ndim)]) for position in (source, target)]
    chosen = jax.random.permutation(own_key, parts)[partner]
    strong = (owner == chosen) | (owner == (partner + parts // 2) % parts)
    return jnp.where(strong, factor * entries, entries)


def levels(key, shape, shards, least, top_value):
    gain = 1.0
    for axis_at, blocks in shards:
        steps = jax.random.uniform(jax.random.fold_in(jax.random.fold_in(key, 6), axis_at), (blocks,), jnp.float32, least / len(shards), top_value / len(shards))
        gain = gain * jnp.repeat(jnp.exp(steps), shape[axis_at] // blocks).reshape((-1,) + (1,) * (len(shape) - 1 - axis_at))
    return gain


def gaussian(rng, dims, spread, most, cuts=(), held_as=jnp.bfloat16):
    loudness = levels(rng, dims, cuts, -0.22, 0.18) if cuts else 1.0
    result = jax.random.normal(rng, dims, jnp.float32) * spread * loudness
    return jnp.minimum(jnp.maximum(result, -most), most).astype(held_as)


def noise_with(own_key, extent, width, most, shards, heavy, kind=jnp.bfloat16):
    drawn = width * jax.random.normal(own_key, extent, jnp.float32)
    if shards:
        drawn = drawn * levels(own_key, extent, shards, -0.22, 0.18)
    return jnp.clip(spiked(drawn, jax.random.fold_in(own_key, 3), *heavy), -most, most).astype(kind)


def setup_inputs(seed: int = 0) -> dict:
    key_list = jax.random.split(jax.random.key(seed), 7)
    return {
        "text_query": draw_text_query(jax.random.fold_in(key_list[6], 71), 0),
        "vision_key": draw_vision_key(jax.random.fold_in(key_list[6], 71), 0),
        "vision_value": gaussian(key_list[2], (VISION, KV_HEADS * HEAD), 1.0, 6.0, ((0, 64), (1, 8))),
        "grad_output": gaussian(key_list[3], (TEXT, Q_HEADS * HEAD), 32.0, 192.0, ((0, 64), (1, 8))),
        "key_weight": noise_with(key_list[4], (VIS_WIDTH, KV_HEADS * HEAD), VIS_WIDTH ** -0.5, 0.1875, ((0, 64), (1, 8)), (1, 0, 64, 4.0)),
        "value_weight": noise_with(key_list[5], (VIS_WIDTH, KV_HEADS * HEAD), VIS_WIDTH ** -0.5, 0.1875, ((0, 64), (1, 8)), (1, 0, 64, 4.0)),
    }


def reference(text_query, vision_key, vision_value, grad_output, key_weight, value_weight):
    scaling = 1.0 / math.sqrt(HEAD)
    query_heads = text_query.reshape(TEXT, Q_HEADS, HEAD).transpose(1, 0, 2)
    output_heads = grad_output.reshape(TEXT, Q_HEADS, HEAD).transpose(1, 0, 2)
    key_heads = vision_key.reshape(VISION, KV_HEADS, HEAD).transpose(1, 0, 2)
    value_heads = vision_value.reshape(VISION, KV_HEADS, HEAD).transpose(1, 0, 2)
    group_ids = (jnp.arange(Q_HEADS, dtype=jnp.int32) // QPG).astype(jnp.int32)

    def single_head(inputs):
        query_one, output_one, group_id = inputs
        key_one = lax.dynamic_index_in_dim(key_heads, group_id, 0, keepdims=False)
        value_one = lax.dynamic_index_in_dim(value_heads, group_id, 0, keepdims=False)
        logits = jnp.dot(query_one, key_one.T, preferred_element_type=jnp.float32) * scaling
        row_max = lax.optimization_barrier(jnp.max(logits, axis=1, keepdims=True))
        exponent = jnp.exp(logits - row_max)
        row_sums = lax.optimization_barrier(jnp.sum(exponent, axis=1, keepdims=True))
        attention = exponent / row_sums
        grad_probs = jnp.dot(output_one, value_one.T, preferred_element_type=jnp.float32)
        row_dots = lax.optimization_barrier(jnp.sum(attention * grad_probs, axis=1, keepdims=True))
        value_term = jnp.dot(attention.astype(jnp.bfloat16).T, output_one, preferred_element_type=jnp.float32)
        grad_logits = (attention * (grad_probs - row_dots) * scaling).astype(jnp.bfloat16)
        query_term = jnp.dot(grad_logits, key_one, preferred_element_type=jnp.float32).astype(jnp.bfloat16)
        key_term = jnp.dot(grad_logits.T, query_one, preferred_element_type=jnp.float32)
        return (query_term, key_term, value_term)
    query_terms, key_terms, value_terms = lax.map(single_head, (query_heads, output_heads, group_ids))
    grad_query = query_terms.transpose(1, 0, 2).reshape(TEXT, Q_HEADS * HEAD)
    grad_key = key_terms.reshape(KV_HEADS, QPG, VISION, HEAD).sum(axis=1)
    grad_key = grad_key.transpose(1, 0, 2).reshape(VISION, KV_HEADS * HEAD).astype(jnp.bfloat16)
    grad_value = value_terms.reshape(KV_HEADS, QPG, VISION, HEAD).sum(axis=1)
    grad_value = grad_value.transpose(1, 0, 2).reshape(VISION, KV_HEADS * HEAD).astype(jnp.bfloat16)
    grad_vision = jnp.dot(grad_key, key_weight.T, preferred_element_type=jnp.float32)
    grad_vision = grad_vision + jnp.dot(grad_value, value_weight.T, preferred_element_type=jnp.float32)
    return (grad_query, grad_vision.astype(jnp.bfloat16))
```

```python
import math

import jax
import jax.numpy as jnp
from jax import lax
from jax.experimental import pallas as pl
from jax.experimental.pallas import tpu as pltpu
from jax.sharding import PartitionSpec as P

HEAD = 128
SCALING = 1.0 / math.sqrt(HEAD)
EXP2_SCALE = SCALING * math.log2(math.e)
LANES = 256
MESH = pl.DeviceIdType.MESH
F32 = jnp.float32
BF16 = jnp.bfloat16


def contract_last(a, b):
    return lax.dot_general(a, b, (((1,), (1,)), ((), ())), preferred_element_type=F32)


def kernel(
    sizes,
    query_ref, key_ref, value_ref, upstream_ref, key_weight_ref, value_weight_ref,
    grad_query_ref, grad_vision_ref,
    pairs, weights, query_rows, upstream_rows, query_t, upstream_t,
    exps, probs_grad, chunk_max, run_max, run_sum, run_dot,
    attn_low, logit_low, query_grad_t,
    term_send, term_recv, own_sum, row_send, row_recv, gathered,
    projected, sib_send, sib_recv, fin_send, fin_recv,
    gy_send, gy_recv, gu_send, gu_recv, wy_send, wy_recv,
    ru_send, ru_recv, ry_send, ry_recv, au_send, au_recv,
    sb_send, sb_recv, fn_send, fn_recv,
):
    nu, ny, nk = sizes
    block = key_ref.shape[0]
    chunk = block * ny
    tokens = query_ref.shape[0]
    heads = query_ref.shape[1] // HEAD
    rows = tokens * heads
    wblock = key_weight_ref.shape[0]
    half = nu // 2
    s = lax.axis_index("seq")
    g = lax.axis_index("kv")
    u, y = s // ny, s % ny
    core, pair = g % 2, g // 2
    diag = jnp.where(u == g, 1, 0)

    def at(u_, y_, g_):
        return {"seq": u_ * ny + y_, "kv": g_}

    def u_peer(d):
        return at((u + d) % nu, y, g)

    def y_peer(d):
        return at(u, (y + d) % ny, g)

    sibling = at(u, y, g + 1 - 2 * core)

    def remote(src, dst, send, recv, device):
        return pltpu.make_async_remote_copy(
            src_ref=src, dst_ref=dst, send_sem=send, recv_sem=recv,
            device_id=device, device_id_type=MESH,
        )

    barrier = pltpu.get_barrier_semaphore()

    def greet(device):
        pl.semaphore_signal(barrier, inc=1, device_id=device, device_id_type=MESH)

    @pl.loop(1, ny)
    def _(d):
        greet(y_peer(d))

    @pl.loop(1, nu)
    def _(d):
        greet(u_peer(d))

    greet(sibling)

    @pl.loop(0, nk // 2)
    def _(j):
        source = 2 * j + u % 2

        @pl.when(jnp.logical_not((u == g) & (source == g)))
        def _():
            greet(at(g, y, source))

    own_rows = pl.ds(pl.multiple_of(s * block, block), block)
    pairs[own_rows, :HEAD] = key_ref[...]
    pairs[own_rows, HEAD:] = value_ref[...]
    own_w = pl.ds(pl.multiple_of(y * wblock, wblock), wblock)
    weights[own_w, :HEAD] = key_weight_ref[...]
    weights[own_w, HEAD:] = value_weight_ref[...]
    for h in range(heads):
        at_cols = pl.ds(h * HEAD, HEAD)
        at_rows = pl.ds(h * tokens, tokens)
        q = query_ref[:, at_cols]
        o = upstream_ref[:, at_cols]
        query_rows[at_rows, :] = q
        upstream_rows[at_rows, :] = o
        query_t[:, at_rows] = q.T
        upstream_t[:, at_rows] = o.T
    run_max[...] = jnp.full_like(run_max, -1e30)
    run_sum[...] = jnp.zeros_like(run_sum)
    run_dot[...] = jnp.zeros_like(run_dot)
    query_grad_t[...] = jnp.zeros_like(query_grad_t)

    pl.semaphore_wait(barrier, (ny - 1) + (nu - 1) + 1 + half - diag)

    def gather_y(d):
        return remote(pairs.at[own_rows], pairs.at[own_rows], gy_send.at[d], gy_recv.at[d], y_peer(d))

    @pl.loop(1, ny)
    def _(d):
        gather_y(d).start()

    @pl.loop(1, ny)
    def _(d):
        gather_y(d).wait_recv()

    u_rows = pl.ds(pl.multiple_of(u * chunk, chunk), chunk)

    def gather_u(d):
        return remote(pairs.at[u_rows], pairs.at[u_rows], gu_send.at[d], gu_recv.at[d], u_peer(d))

    @pl.loop(1, nu)
    def _(d):
        gather_u(d).start()

    def gather_w(d):
        return remote(weights.at[own_w], weights.at[own_w], wy_send.at[d], wy_recv.at[d], y_peer(d))

    @pl.loop(1, ny)
    def _(d):
        gather_w(d).start()

    @pl.loop(0, nu)
    def _(d):
        @pl.when(d > 0)
        def _():
            gather_u(d).wait_recv()

        c = (u - d + nu) % nu
        at_c = pl.ds(pl.multiple_of(c * chunk, chunk), chunk)
        keys = pairs[at_c, :HEAD]
        values = pairs[at_c, HEAD:]
        for n in range(rows // LANES):
            cols = pl.ds(n * LANES, LANES)
            logits = jnp.dot(keys, query_t[:, cols], preferred_element_type=F32)
            gp = jnp.dot(values, upstream_t[:, cols], preferred_element_type=F32)
            old = run_max[:, cols]
            new = jnp.maximum(old, jnp.max(logits, axis=0, keepdims=True))
            factor = jnp.exp2((old - new) * EXP2_SCALE)
            e = jnp.exp2((logits - new) * EXP2_SCALE)
            run_max[:, cols] = new
            run_sum[:, cols] = run_sum[:, cols] * factor + jnp.sum(e, axis=0, keepdims=True)
            run_dot[:, cols] = run_dot[:, cols] * factor + jnp.sum(e * gp, axis=0, keepdims=True)
            exps[at_c, cols] = e
            probs_grad[at_c, cols] = gp
            chunk_max[c, :, cols] = new

    run_sum[...] = 1.0 / run_sum[...]
    run_dot[...] = run_dot[...] * run_sum[...]

    def reduce_u(d):
        return remote(term_send.at[d], term_recv.at[d], ru_send.at[d], ru_recv.at[d], u_peer(d))

    @pl.loop(1, nu + 1)
    def _(d):
        c = (u + d) % nu
        at_c = pl.ds(pl.multiple_of(c * chunk, chunk), chunk)
        for n in range(rows // LANES):
            cols = pl.ds(n * LANES, LANES)
            share = (
                jnp.exp2((chunk_max[c, :, cols] - run_max[:, cols]) * EXP2_SCALE)
                * run_sum[:, cols]
            )
            a = exps[at_c, cols] * share
            attn_low[:, cols] = a.astype(BF16)
            logit_low[:, cols] = (
                a * (probs_grad[at_c, cols] - run_dot[:, cols]) * SCALING
            ).astype(BF16)
        key_term = jnp.dot(logit_low[...], query_rows[...], preferred_element_type=F32)
        value_term = jnp.dot(attn_low[...], upstream_rows[...], preferred_element_type=F32)

        @pl.when(d < nu)
        def _():
            term_send[d, :, :HEAD] = key_term.astype(BF16)
            term_send[d, :, HEAD:] = value_term.astype(BF16)
            reduce_u(d).start()

        @pl.when(d == nu)
        def _():
            own_sum[:, :HEAD] = key_term
            own_sum[:, HEAD:] = value_term

        keys_t = pairs[at_c, :HEAD].T
        query_grad_t[...] += jnp.dot(keys_t, logit_low[...], preferred_element_type=F32)

    for h in range(heads):
        grad_query_ref[:, pl.ds(h * HEAD, HEAD)] = (
            query_grad_t[:, pl.ds(h * tokens, tokens)].T.astype(BF16)
        )

    @pl.loop(1, nu)
    def _(d):
        reduce_u(d).wait_recv()
        own_sum[...] += term_recv[d].astype(F32)

    def reduce_y(d):
        return remote(row_send.at[d], row_recv.at[d], ry_send.at[d], ry_recv.at[d], y_peer(d))

    def y_rows(d):
        return pl.ds(pl.multiple_of(((y + d) % ny) * block, block), block)

    @pl.loop(1, ny)
    def _(d):
        row_send[d] = own_sum[y_rows(d), :].astype(BF16)
        reduce_y(d).start()

    owned = own_sum[y_rows(0), :]
    for d in range(1, ny):
        reduce_y(d).wait_recv()
        owned += row_recv[d].astype(F32)
    gathered[u] = owned.astype(BF16)

    def spread_u(d):
        return remote(gathered.at[u], gathered.at[u], au_send.at[d], au_recv.at[d], u_peer(d))

    @pl.loop(1, nu)
    def _(d):
        spread_u(d).start()

    @pl.loop(1, ny)
    def _(d):
        gather_w(d).wait_recv()

    @pl.loop(1, nu)
    def _(d):
        spread_u(d).wait_recv()

    grads = gathered[...].reshape(nu * block, 2 * HEAD)
    for n in range(ny * wblock // LANES):
        cols = pl.ds(n * LANES, LANES)
        projected[:, cols] = contract_last(grads, weights[cols, :])

    def part(j, parity):
        return pl.ds(pl.multiple_of((2 * j + parity) * block, block), block)

    def swap(j):
        return remote(sib_send.at[j], sib_recv.at[j], sb_send.at[j], sb_recv.at[j], sibling)

    @pl.loop(0, half)
    def _(j):
        sib_send[j] = projected[part(j, 1 - core), :].astype(BF16)
        swap(j).start()

    def finish(j):
        return remote(
            fin_send.at[j], fin_recv.at[pair], fn_send.at[j], fn_recv.at[pair],
            at(2 * j + core, y, u),
        )

    def to_self(j):
        return (u == g) & (2 * j + core == u)

    @pl.loop(0, half)
    def _(j):
        swap(j).wait_recv()
        total = projected[part(j, core), :] + sib_recv[j].astype(F32)
        fin_send[j] = total.astype(BF16)

        @pl.when(jnp.logical_not(to_self(j)))
        def _():
            finish(j).start()

        @pl.when(to_self(j))
        def _():
            fin_recv[pair] = total.astype(BF16)

    @pl.loop(0, nk // 2)
    def _(j):
        @pl.when(jnp.logical_not((u == g) & (j == pair)))
        def _():
            remote(
                fin_send.at[0], fin_recv.at[j], fn_send.at[0], fn_recv.at[j], sibling
            ).wait_recv()

    result = fin_recv[0].astype(F32)
    for j in range(1, nk // 2):
        result += fin_recv[j].astype(F32)
    grad_vision_ref[...] = result.astype(BF16)

    @pl.loop(1, ny)
    def _(d):
        gather_y(d).wait_send()
        gather_w(d).wait_send()
        reduce_y(d).wait_send()

    @pl.loop(1, nu)
    def _(d):
        gather_u(d).wait_send()
        reduce_u(d).wait_send()
        spread_u(d).wait_send()

    @pl.loop(0, half)
    def _(j):
        swap(j).wait_send()

        @pl.when(jnp.logical_not(to_self(j)))
        def _():
            finish(j).wait_send()


def shards(sizes, text_query, vision_key, vision_value, grad_output, key_weight, value_weight):
    nu, ny, nk = sizes
    block = vision_key.shape[0]
    chunk = block * ny
    keys = chunk * nu
    tokens = text_query.shape[0]
    heads = text_query.shape[1] // HEAD
    rows = tokens * heads
    wide = key_weight.shape[0] * ny
    half = nu // 2
    vmem = pltpu.VMEM
    dma = pltpu.SemaphoreType.DMA
    return pl.pallas_call(
        lambda *refs: kernel(sizes, *refs),
        out_shape=(
            jax.ShapeDtypeStruct(text_query.shape, BF16),
            jax.ShapeDtypeStruct((block, wide), BF16),
        ),
        in_specs=[pl.BlockSpec(memory_space=pltpu.VMEM)] * 6,
        out_specs=(pl.BlockSpec(memory_space=pltpu.VMEM),) * 2,
        scratch_shapes=[
            vmem((keys, 2 * HEAD), BF16),
            vmem((wide, 2 * HEAD), BF16),
            vmem((rows, HEAD), BF16),
            vmem((rows, HEAD), BF16),
            vmem((HEAD, rows), BF16),
            vmem((HEAD, rows), BF16),
            vmem((keys, rows), F32),
            vmem((keys, rows), F32),
            vmem((nu, 1, rows), F32),
            vmem((1, rows), F32),
            vmem((1, rows), F32),
            vmem((1, rows), F32),
            vmem((chunk, rows), BF16),
            vmem((chunk, rows), BF16),
            vmem((HEAD, rows), F32),
            vmem((nu, chunk, 2 * HEAD), BF16),
            vmem((nu, chunk, 2 * HEAD), BF16),
            vmem((chunk, 2 * HEAD), F32),
            vmem((ny, block, 2 * HEAD), BF16),
            vmem((ny, block, 2 * HEAD), BF16),
            vmem((nu, block, 2 * HEAD), BF16),
            vmem((nu * block, wide), F32),
            vmem((half, block, wide), BF16),
            vmem((half, block, wide), BF16),
            vmem((half, block, wide), BF16),
            vmem((nk // 2, block, wide), BF16),
            dma((ny,)), dma((ny,)), dma((nu,)), dma((nu,)), dma((ny,)), dma((ny,)),
            dma((nu,)), dma((nu,)), dma((ny,)), dma((ny,)), dma((nu,)), dma((nu,)),
            dma((half,)), dma((half,)), dma((half,)), dma((nk // 2,)),
        ],
        compiler_params=pltpu.CompilerParams(
            collective_id=0, has_side_effects=True, vmem_limit_bytes=48 * 1024 * 1024
        ),
    )(text_query, vision_key, vision_value, grad_output, key_weight, value_weight)


def solution(mesh):
    nk = mesh.shape["kv"]
    sizes = (nk, mesh.shape["seq"] // nk, nk)
    spec = P("seq", "kv")
    return jax.shard_map(
        lambda *arrays: shards(sizes, *arrays),
        mesh=mesh,
        in_specs=(spec,) * 6,
        out_specs=(spec, spec),
        check_vma=False,
    )
```

```python
import math

import jax
import jax.numpy as jnp
from jax import lax
from jax.experimental import pallas as pl
from jax.experimental.pallas import tpu as pltpu
from jax.sharding import PartitionSpec as P

HEAD = 128
SCALING = 1.0 / math.sqrt(HEAD)
EXP2_SCALE = SCALING * math.log2(math.e)
LANES = 256
MESH = pl.DeviceIdType.MESH
F32 = jnp.float32
BF16 = jnp.bfloat16


def contract_last(a, b):
    return lax.dot_general(a, b, (((1,), (1,)), ((), ())), preferred_element_type=F32)


def kernel(
    sizes,
    query_ref, key_ref, value_ref, upstream_ref, key_weight_ref, value_weight_ref,
    grad_query_ref, grad_vision_ref,
    pairs, weights, query_rows, upstream_rows, query_t, upstream_t,
    exps, probs_grad, chunk_max, run_max, run_sum, run_dot,
    attn_low, logit_low, query_grad_t,
    term_send, term_recv, own_sum, row_send, row_recv, own_low, gathered,
    fin_send, fin_recv, query_in, upstream_in,
    gy_send, gy_recv, gu_send, gu_recv, wy_send, wy_recv,
    ru_send, ru_recv, ry_send, ry_recv, au_send, au_recv,
    fn_send, fn_recv, sb_send, sb_recv, in_sem,
):
    nu, ny, nk = sizes
    block = key_ref.shape[0]
    chunk = block * ny
    tokens = query_ref.shape[0]
    heads = query_ref.shape[1] // HEAD
    rows = tokens * heads
    wblock = key_weight_ref.shape[0]
    half = nu // 2
    s = lax.axis_index("seq")
    g = lax.axis_index("kv")
    u, y = s // ny, s % ny
    core, pair = g % 2, g // 2
    diag = jnp.where(u == g, 1, 0)

    def at(u_, y_, g_):
        return {"seq": u_ * ny + y_, "kv": g_}

    def u_peer(d):
        return at((u + d) % nu, y, g)

    def y_peer(d):
        return at(u, (y + d) % ny, g)

    def spread_to(d):
        return at((u + d) % nu, y, 2 * pair + u % 2)

    sibling = at(u, y, g + 1 - 2 * core)
    lead = core == u % 2

    def remote(src, dst, send, recv, device):
        return pltpu.make_async_remote_copy(
            src_ref=src, dst_ref=dst, send_sem=send, recv_sem=recv,
            device_id=device, device_id_type=MESH,
        )

    own_rows = pl.ds(pl.multiple_of(s * block, block), block)
    own_w = pl.ds(pl.multiple_of(y * wblock, wblock), wblock)
    left, right = slice(0, HEAD), slice(HEAD, 2 * HEAD)
    loads = [
        pltpu.make_async_copy(src, dst, in_sem.at[i])
        for i, (src, dst) in enumerate((
            (key_ref, pairs.at[own_rows, left]),
            (value_ref, pairs.at[own_rows, right]),
            (query_ref, query_in),
            (upstream_ref, upstream_in),
            (key_weight_ref, weights.at[core, own_w, left]),
            (value_weight_ref, weights.at[core, own_w, right]),
        ))
    ]
    for load in loads:
        load.start()

    barrier = pltpu.get_barrier_semaphore()

    def greet(device):
        pl.semaphore_signal(barrier, inc=1, device_id=device, device_id_type=MESH)

    @pl.loop(1, ny)
    def _(d):
        greet(y_peer(d))

    @pl.loop(1, nu)
    def _(d):
        greet(u_peer(d))

    greet(sibling)

    @pl.loop(0, half)
    def _(k):
        for c in range(2):
            @pl.when(jnp.logical_not((2 * k + core == u) & (core == c)))
            def _():
                greet(at(2 * k + core, y, 2 * pair + c))

    @pl.loop(0, nk // 2)
    def _(j):
        source = 2 * j + u % 2

        @pl.when(jnp.logical_not((u == g) & (source == g)))
        def _():
            greet(at(g, y, source))

    loads[0].wait()
    loads[1].wait()
    pl.semaphore_wait(
        barrier, (ny - 1) + (nu - 1) + 1 + nu - jnp.where(lead, 1, 0) + half - diag
    )

    def gather_y(d):
        return remote(pairs.at[own_rows], pairs.at[own_rows], gy_send.at[d], gy_recv.at[d], y_peer(d))

    @pl.loop(1, ny)
    def _(d):
        gather_y(d).start()

    loads[2].wait()
    loads[3].wait()
    for h in range(heads):
        at_cols = pl.ds(h * HEAD, HEAD)
        at_rows = pl.ds(h * tokens, tokens)
        q = query_in[:, at_cols]
        o = upstream_in[:, at_cols]
        query_rows[at_rows, :] = q
        upstream_rows[at_rows, :] = o
        query_t[:, at_rows] = q.T
        upstream_t[:, at_rows] = o.T
    run_max[...] = jnp.full_like(run_max, -1e30)
    run_sum[...] = jnp.zeros_like(run_sum)
    run_dot[...] = jnp.zeros_like(run_dot)
    query_grad_t[...] = jnp.zeros_like(query_grad_t)
    loads[4].wait()
    loads[5].wait()

    @pl.loop(1, ny)
    def _(d):
        gather_y(d).wait_recv()

    u_rows = pl.ds(pl.multiple_of(u * chunk, chunk), chunk)

    def gather_u(d):
        return remote(pairs.at[u_rows], pairs.at[u_rows], gu_send.at[d], gu_recv.at[d], u_peer(d))

    @pl.loop(1, nu)
    def _(d):
        gather_u(d).start()

    def gather_w(d):
        own = weights.at[core, own_w]
        return remote(own, own, wy_send.at[d], wy_recv.at[d], y_peer(d))

    @pl.loop(1, ny)
    def _(d):
        gather_w(d).start()

    @pl.loop(0, nu)
    def _(d):
        @pl.when(d > 0)
        def _():
            gather_u(d).wait_recv()

        c = (u - d + nu) % nu
        at_c = pl.ds(pl.multiple_of(c * chunk, chunk), chunk)
        keys = pairs[at_c, :HEAD]
        values = pairs[at_c, HEAD:]
        for n in range(rows // LANES):
            cols = pl.ds(n * LANES, LANES)
            logits = jnp.dot(keys, query_t[:, cols], preferred_element_type=F32)
            gp = jnp.dot(values, upstream_t[:, cols], preferred_element_type=F32)
            old = run_max[:, cols]
            new = jnp.maximum(old, jnp.max(logits, axis=0, keepdims=True))
            factor = jnp.exp2((old - new) * EXP2_SCALE)
            e = jnp.exp2((logits - new) * EXP2_SCALE)
            run_max[:, cols] = new
            run_sum[:, cols] = run_sum[:, cols] * factor + jnp.sum(e, axis=0, keepdims=True)
            run_dot[:, cols] = run_dot[:, cols] * factor + jnp.sum(e * gp, axis=0, keepdims=True)
            exps[at_c, cols] = e
            probs_grad[at_c, cols] = gp
            chunk_max[c, :, cols] = new

    run_sum[...] = 1.0 / run_sum[...]
    run_dot[...] = run_dot[...] * run_sum[...]

    def reduce_u(d):
        return remote(term_send.at[d], term_recv.at[d], ru_send.at[d], ru_recv.at[d], u_peer(d))

    @pl.loop(1, nu + 1)
    def _(d):
        c = (u + d) % nu
        at_c = pl.ds(pl.multiple_of(c * chunk, chunk), chunk)
        for n in range(rows // LANES):
            cols = pl.ds(n * LANES, LANES)
            share = (
                jnp.exp2((chunk_max[c, :, cols] - run_max[:, cols]) * EXP2_SCALE)
                * run_sum[:, cols]
            )
            a = exps[at_c, cols] * share
            attn_low[:, cols] = a.astype(BF16)
            logit_low[:, cols] = (
                a * (probs_grad[at_c, cols] - run_dot[:, cols]) * SCALING
            ).astype(BF16)
        key_term = jnp.dot(logit_low[...], query_rows[...], preferred_element_type=F32)
        value_term = jnp.dot(attn_low[...], upstream_rows[...], preferred_element_type=F32)

        @pl.when(d < nu)
        def _():
            term_send[d, :, :HEAD] = key_term.astype(BF16)
            term_send[d, :, HEAD:] = value_term.astype(BF16)
            reduce_u(d).start()

        @pl.when(d == nu)
        def _():
            own_sum[:, :HEAD] = key_term
            own_sum[:, HEAD:] = value_term

        keys_t = pairs[at_c, :HEAD].T
        query_grad_t[...] += jnp.dot(keys_t, logit_low[...], preferred_element_type=F32)

    for h in range(heads):
        grad_query_ref[:, pl.ds(h * HEAD, HEAD)] = (
            query_grad_t[:, pl.ds(h * tokens, tokens)].T.astype(BF16)
        )

    @pl.loop(1, ny)
    def _(d):
        gather_w(d).wait_recv()

    share_w = remote(
        weights.at[core], weights.at[core], sb_send.at[0], sb_recv.at[0], sibling
    )
    share_w.start()

    @pl.loop(1, nu)
    def _(d):
        reduce_u(d).wait_recv()
        own_sum[...] += term_recv[d].astype(F32)

    def reduce_y(d):
        return remote(row_send.at[d], row_recv.at[d], ry_send.at[d], ry_recv.at[d], y_peer(d))

    def y_rows(d):
        return pl.ds(pl.multiple_of(((y + d) % ny) * block, block), block)

    @pl.loop(1, ny)
    def _(d):
        row_send[d] = own_sum[y_rows(d), :].astype(BF16)
        reduce_y(d).start()

    owned = own_sum[y_rows(0), :]
    for d in range(1, ny):
        reduce_y(d).wait_recv()
        owned += row_recv[d].astype(F32)
    own_low[...] = owned.astype(BF16)

    def spread_u(d):
        return remote(
            own_low, gathered.at[core, u // 2], au_send.at[d], au_recv.at[core * half + u // 2], spread_to(d)
        )

    @pl.when(lead)
    def _():
        gathered[core, u // 2] = own_low[...]

    @pl.when(jnp.logical_not(lead))
    def _():
        spread_u(0).start()

    @pl.loop(1, nu)
    def _(d):
        spread_u(d).start()

    share_w.wait_recv()

    @pl.loop(0, half)
    def _(k):
        for c in range(2):
            @pl.when(jnp.logical_not((2 * k + core == u) & (core == c)))
            def _():
                slot = gathered.at[c, k]
                remote(
                    slot, slot, au_send.at[0], au_recv.at[c * half + k], sibling
                ).wait_recv()

    for n in range(ny * wblock // LANES):
        cols = pl.ds(n * LANES, LANES)
        total = sum(
            contract_last(gathered[c].reshape(half * block, 2 * HEAD), weights[c, cols, :])
            for c in range(2)
        )
        fin_send[:, :, cols] = total.astype(BF16).reshape(half, block, LANES)

    def finish(j):
        return remote(
            fin_send.at[j], fin_recv.at[pair], fn_send.at[j], fn_recv.at[pair],
            at(2 * j + core, y, u),
        )

    def to_self(j):
        return (u == g) & (2 * j + core == u)

    @pl.loop(0, half)
    def _(j):
        @pl.when(jnp.logical_not(to_self(j)))
        def _():
            finish(j).start()

        @pl.when(to_self(j))
        def _():
            fin_recv[pair] = fin_send[j]

    @pl.loop(0, nk // 2)
    def _(j):
        @pl.when(jnp.logical_not((u == g) & (j == pair)))
        def _():
            remote(
                fin_send.at[0], fin_recv.at[j], fn_send.at[0], fn_recv.at[j], sibling
            ).wait_recv()

    result = fin_recv[0].astype(F32)
    for j in range(1, nk // 2):
        result += fin_recv[j].astype(F32)
    grad_vision_ref[...] = result.astype(BF16)

    @pl.loop(1, ny)
    def _(d):
        gather_y(d).wait_send()
        gather_w(d).wait_send()
        reduce_y(d).wait_send()

    @pl.loop(1, nu)
    def _(d):
        gather_u(d).wait_send()
        reduce_u(d).wait_send()
        spread_u(d).wait_send()

    @pl.when(jnp.logical_not(lead))
    def _():
        spread_u(0).wait_send()

    share_w.wait_send()

    @pl.loop(0, half)
    def _(j):
        @pl.when(jnp.logical_not(to_self(j)))
        def _():
            finish(j).wait_send()


def shards(sizes, text_query, vision_key, vision_value, grad_output, key_weight, value_weight):
    nu, ny, nk = sizes
    block = vision_key.shape[0]
    chunk = block * ny
    keys = chunk * nu
    tokens = text_query.shape[0]
    heads = text_query.shape[1] // HEAD
    rows = tokens * heads
    wide = key_weight.shape[0] * ny
    half = nu // 2
    vmem = pltpu.VMEM
    dma = pltpu.SemaphoreType.DMA
    return pl.pallas_call(
        lambda *refs: kernel(sizes, *refs),
        out_shape=(
            jax.ShapeDtypeStruct(text_query.shape, BF16),
            jax.ShapeDtypeStruct((block, wide), BF16),
        ),
        in_specs=[pl.BlockSpec(memory_space=pltpu.HBM)] * 6,
        out_specs=(pl.BlockSpec(memory_space=pltpu.VMEM),) * 2,
        scratch_shapes=[
            vmem((keys, 2 * HEAD), BF16),
            vmem((2, wide, 2 * HEAD), BF16),
            vmem((rows, HEAD), BF16),
            vmem((rows, HEAD), BF16),
            vmem((HEAD, rows), BF16),
            vmem((HEAD, rows), BF16),
            vmem((keys, rows), F32),
            vmem((keys, rows), F32),
            vmem((nu, 1, rows), F32),
            vmem((1, rows), F32),
            vmem((1, rows), F32),
            vmem((1, rows), F32),
            vmem((chunk, rows), BF16),
            vmem((chunk, rows), BF16),
            vmem((HEAD, rows), F32),
            vmem((nu, chunk, 2 * HEAD), BF16),
            vmem((nu, chunk, 2 * HEAD), BF16),
            vmem((chunk, 2 * HEAD), F32),
            vmem((ny, block, 2 * HEAD), BF16),
            vmem((ny, block, 2 * HEAD), BF16),
            vmem((block, 2 * HEAD), BF16),
            vmem((2, half, block, 2 * HEAD), BF16),
            vmem((half, block, wide), BF16),
            vmem((nk // 2, block, wide), BF16),
            vmem(text_query.shape, BF16),
            vmem(text_query.shape, BF16),
            dma((ny,)), dma((ny,)), dma((nu,)), dma((nu,)), dma((ny,)), dma((ny,)),
            dma((nu,)), dma((nu,)), dma((ny,)), dma((ny,)), dma((nu,)), dma((nu,)),
            dma((half,)), dma((nk // 2,)), dma((1,)), dma((1,)), dma((6,)),
        ],
        compiler_params=pltpu.CompilerParams(
            collective_id=0, has_side_effects=True, vmem_limit_bytes=60 * 1024 * 1024
        ),
    )(text_query, vision_key, vision_value, grad_output, key_weight, value_weight)


def solution(mesh):
    nk = mesh.shape["kv"]
    sizes = (nk, mesh.shape["seq"] // nk, nk)
    spec = P("seq", "kv")
    return jax.shard_map(
        lambda *arrays: shards(sizes, *arrays),
        mesh=mesh,
        in_specs=(spec,) * 6,
        out_specs=(spec, spec),
        check_vma=False,
    )
```

```python
import math

import jax
import jax.numpy as jnp
from jax import lax
from jax.experimental import pallas as pl
from jax.experimental.pallas import tpu as pltpu
from jax.sharding import PartitionSpec as P

HEAD = 128
SCALING = 1.0 / math.sqrt(HEAD)
EXP2_SCALE = SCALING * math.log2(math.e)
LANES = 256
PARTS = 2
MESH = pl.DeviceIdType.MESH
F32 = jnp.float32
BF16 = jnp.bfloat16


def contract_last(a, b):
    return lax.dot_general(a, b, (((1,), (1,)), ((), ())), preferred_element_type=F32)


def kernel(
    sizes,
    query_ref, key_ref, value_ref, upstream_ref, key_weight_ref, value_weight_ref,
    grad_query_ref, grad_vision_ref,
    pairs, weights, query_rows, upstream_rows, query_t, upstream_t,
    exps, probs_grad, chunk_max, run_max, run_sum, run_dot,
    attn_low, logit_low, query_grad_t,
    term_send, term_recv, own_sum, row_send, row_recv, own_low, gathered,
    fin_send, fin_recv, query_in, upstream_in,
    gy_send, gy_recv, gu_send, gu_recv, wy_send, wy_recv,
    ru_send, ru_recv, ry_send, ry_recv, au_send, au_recv,
    fn_send, fn_recv, sb_send, sb_recv, in_sem,
):
    nu, ny, nk = sizes
    block = key_ref.shape[0]
    chunk = block * ny
    tokens = query_ref.shape[0]
    heads = query_ref.shape[1] // HEAD
    rows = tokens * heads
    wblock = key_weight_ref.shape[0]
    half = nu // 2
    s = lax.axis_index("seq")
    g = lax.axis_index("kv")
    u, y = s // ny, s % ny
    core, pair = g % 2, g // 2
    diag = jnp.where(u == g, 1, 0)

    def at(u_, y_, g_):
        return {"seq": u_ * ny + y_, "kv": g_}

    def u_peer(d):
        return at((u + d) % nu, y, g)

    def y_peer(d):
        return at(u, (y + d) % ny, g)

    def spread_to(d):
        return at((u + d) % nu, y, 2 * pair + u % 2)

    sibling = at(u, y, g + 1 - 2 * core)
    lead = core == u % 2

    def remote(src, dst, send, recv, device):
        return pltpu.make_async_remote_copy(
            src_ref=src, dst_ref=dst, send_sem=send, recv_sem=recv,
            device_id=device, device_id_type=MESH,
        )

    order = [0]
    for step in range(1, ny // 2 + 1):
        order += [r for r in (step, ny - step) if r not in order]
    groups = [(0, 1), (1, min(3, ny)), (min(3, ny), ny)]
    groups = [(lo, hi) for lo, hi in groups if hi > lo]

    def slots(lo, hi):
        return pl.ds(pl.multiple_of(u * chunk + lo * block, block), (hi - lo) * block)

    own_rows = slots(0, 1)
    own_w = pl.ds(pl.multiple_of(y * wblock, wblock), wblock)
    left, right = slice(0, HEAD), slice(HEAD, 2 * HEAD)
    loads = [
        pltpu.make_async_copy(src, dst, in_sem.at[i])
        for i, (src, dst) in enumerate((
            (key_ref, pairs.at[own_rows, left]),
            (value_ref, pairs.at[own_rows, right]),
            (query_ref, query_in),
            (upstream_ref, upstream_in),
            (key_weight_ref, weights.at[core, own_w, left]),
            (value_weight_ref, weights.at[core, own_w, right]),
        ))
    ]
    for load in loads:
        load.start()

    barrier = pltpu.get_barrier_semaphore()

    def greet(device):
        pl.semaphore_signal(barrier, inc=1, device_id=device, device_id_type=MESH)

    @pl.loop(1, ny)
    def _(d):
        greet(y_peer(d))

    @pl.loop(1, nu)
    def _(d):
        greet(u_peer(d))

    greet(sibling)

    @pl.loop(0, half)
    def _(k):
        @pl.when(2 * k + core != u)
        def _():
            greet(at(2 * k + core, y, g + 1 - 2 * core))

    @pl.loop(0, nk // 2)
    def _(j):
        source = 2 * j + u % 2

        @pl.when(jnp.logical_not((u == g) & (source == g)))
        def _():
            greet(at(g, y, source))

    loads[0].wait()
    loads[1].wait()
    pl.semaphore_wait(
        barrier, (ny - 1) + (nu - 1) + 1 + jnp.where(lead, 0, nu - 1) + half - diag
    )

    def gather_y(d):
        i = order.index(ny - d)
        return remote(
            pairs.at[own_rows], pairs.at[slots(i, i + 1)], gy_send.at[d], gy_recv.at[d], y_peer(d)
        )

    def gather_u(d, k):
        part = pairs.at[slots(*groups[k])]
        return remote(part, part, gu_send.at[k, d], gu_recv.at[k, d], u_peer(d))

    for i in reversed(range(1, ny)):
        gather_y(order[i]).start()

    @pl.loop(1, nu)
    def _(d):
        gather_u(d, 0).start()

    loads[2].wait()
    loads[3].wait()
    for h in range(heads):
        at_cols = pl.ds(h * HEAD, HEAD)
        at_rows = pl.ds(h * tokens, tokens)
        q = query_in[:, at_cols]
        o = upstream_in[:, at_cols]
        query_rows[at_rows, :] = q
        upstream_rows[at_rows, :] = o
        query_t[:, at_rows] = q.T
        upstream_t[:, at_rows] = o.T
    run_max[...] = jnp.full_like(run_max, -1e30)
    run_sum[...] = jnp.zeros_like(run_sum)
    run_dot[...] = jnp.zeros_like(run_dot)
    query_grad_t[...] = jnp.zeros_like(query_grad_t)
    loads[4].wait()
    loads[5].wait()

    for k, (lo, hi) in enumerate(groups[1:], 1):
        for i in range(lo, hi):
            gather_y(ny - order[i]).wait_recv()

        @pl.loop(1, nu)
        def _(d):
            gather_u(d, k).start()

    def gather_w(d):
        own = weights.at[core, own_w]
        return remote(own, own, wy_send.at[d], wy_recv.at[d], y_peer(d))

    @pl.loop(1, ny)
    def _(d):
        gather_w(d).start()

    @pl.loop(0, nu)
    def _(d):
        @pl.when(d > 0)
        def _():
            for k in range(len(groups)):
                gather_u(d, k).wait_recv()

        c = (u - d + nu) % nu
        at_c = pl.ds(pl.multiple_of(c * chunk, chunk), chunk)
        keys = pairs[at_c, :HEAD]
        values = pairs[at_c, HEAD:]
        for n in range(rows // LANES):
            cols = pl.ds(n * LANES, LANES)
            logits = jnp.dot(keys, query_t[:, cols], preferred_element_type=F32)
            gp = jnp.dot(values, upstream_t[:, cols], preferred_element_type=F32)
            old = run_max[:, cols]
            new = jnp.maximum(old, jnp.max(logits, axis=0, keepdims=True))
            factor = jnp.exp2((old - new) * EXP2_SCALE)
            e = jnp.exp2((logits - new) * EXP2_SCALE)
            run_max[:, cols] = new
            run_sum[:, cols] = run_sum[:, cols] * factor + jnp.sum(e, axis=0, keepdims=True)
            run_dot[:, cols] = run_dot[:, cols] * factor + jnp.sum(e * gp, axis=0, keepdims=True)
            exps[at_c, cols] = e
            probs_grad[at_c, cols] = gp
            chunk_max[c, :, cols] = new

    run_sum[...] = 1.0 / run_sum[...]
    run_dot[...] = run_dot[...] * run_sum[...]

    span = chunk // PARTS

    def reduce_u(d, h):
        rows_h = pl.ds(pl.multiple_of(h * span, span), span)
        return remote(
            term_send.at[d, rows_h], term_recv.at[d, rows_h],
            ru_send.at[h, d], ru_recv.at[h, d], u_peer(d),
        )

    @pl.loop(0, PARTS * nu)
    def _(t):
        h = PARTS - 1 - t // nu
        d = 1 + t % nu
        c = (u + d) % nu
        at_h = pl.ds(pl.multiple_of(h * span, span), span)
        at_c = pl.ds(pl.multiple_of(c * chunk + h * span, span), span)
        for n in range(rows // LANES):
            cols = pl.ds(n * LANES, LANES)
            share = (
                jnp.exp2((chunk_max[c, :, cols] - run_max[:, cols]) * EXP2_SCALE)
                * run_sum[:, cols]
            )
            a = exps[at_c, cols] * share
            attn_low[:, cols] = a.astype(BF16)
            logit_low[:, cols] = (
                a * (probs_grad[at_c, cols] - run_dot[:, cols]) * SCALING
            ).astype(BF16)
        key_term = jnp.dot(logit_low[...], query_rows[...], preferred_element_type=F32)
        value_term = jnp.dot(attn_low[...], upstream_rows[...], preferred_element_type=F32)

        @pl.when(d < nu)
        def _():
            term_send[d, at_h, left] = key_term.astype(BF16)
            term_send[d, at_h, right] = value_term.astype(BF16)
            reduce_u(d, h).start()

        @pl.when(d == nu)
        def _():
            own_sum[at_h, left] = key_term
            own_sum[at_h, right] = value_term

        keys_t = pairs[at_c, left].T
        query_grad_t[...] += jnp.dot(keys_t, logit_low[...], preferred_element_type=F32)

    for h in range(heads):
        grad_query_ref[:, pl.ds(h * HEAD, HEAD)] = (
            query_grad_t[:, pl.ds(h * tokens, tokens)].T.astype(BF16)
        )

    @pl.loop(1, ny)
    def _(d):
        gather_w(d).wait_recv()

    share_w = remote(
        weights.at[core], weights.at[core], sb_send.at[0], sb_recv.at[0], sibling
    )
    share_w.start()

    def reduce_y(d):
        return remote(row_send.at[d], row_recv.at[d], ry_send.at[d], ry_recv.at[d], y_peer(d))

    for h in reversed(range(PARTS)):
        at_h = pl.ds(h * span, span)

        @pl.loop(1, nu)
        def _(d):
            reduce_u(d, h).wait_recv()
            own_sum[at_h, :] += term_recv[d, at_h, :].astype(F32)

        for i in reversed(range(max(h * ny // PARTS, 1), (h + 1) * ny // PARTS)):
            row_send[order[i]] = own_sum[pl.ds(i * block, block), :].astype(BF16)
            reduce_y(order[i]).start()

    owned = own_sum[pl.ds(0, block), :]
    for i in range(1, ny):
        d = order[i]
        reduce_y(d).wait_recv()
        owned += row_recv[d].astype(F32)
    own_low[...] = owned.astype(BF16)

    def spread_u(d):
        return remote(
            own_low, gathered.at[core, u // 2], au_send.at[d], au_recv.at[core * half + u // 2], spread_to(d)
        )

    @pl.when(lead)
    def _():
        gathered[core, u // 2] = own_low[...]

    @pl.when(jnp.logical_not(lead))
    def _():
        spread_u(0).start()

    @pl.loop(1, nu)
    def _(d):
        spread_u(d).start()

    share_w.wait_recv()

    @pl.loop(0, half)
    def _(k):
        for c in range(2):
            @pl.when(jnp.logical_not((2 * k + core == u) & (core == c)))
            def _():
                slot = gathered.at[c, k]
                remote(
                    slot, slot, au_send.at[0], au_recv.at[c * half + k], sibling
                ).wait_recv()

    for n in range(ny * wblock // LANES):
        cols = pl.ds(n * LANES, LANES)
        total = sum(
            contract_last(gathered[c].reshape(half * block, 2 * HEAD), weights[c, cols, :])
            for c in range(2)
        )
        fin_send[:, :, cols] = total.astype(BF16).reshape(half, block, LANES)

    def finish(j):
        return remote(
            fin_send.at[j], fin_recv.at[pair], fn_send.at[j], fn_recv.at[pair],
            at(2 * j + core, y, u),
        )

    def to_self(j):
        return (u == g) & (2 * j + core == u)

    @pl.loop(0, half)
    def _(j):
        @pl.when(jnp.logical_not(to_self(j)))
        def _():
            finish(j).start()

        @pl.when(to_self(j))
        def _():
            fin_recv[pair] = fin_send[j]

    @pl.loop(0, nk // 2)
    def _(j):
        @pl.when(jnp.logical_not((u == g) & (j == pair)))
        def _():
            remote(
                fin_send.at[0], fin_recv.at[j], fn_send.at[0], fn_recv.at[j], sibling
            ).wait_recv()

    result = fin_recv[0].astype(F32)
    for j in range(1, nk // 2):
        result += fin_recv[j].astype(F32)
    grad_vision_ref[...] = result.astype(BF16)

    for d in range(1, ny):
        gather_y(d).wait_send()
        gather_w(d).wait_send()
        reduce_y(d).wait_send()

    @pl.loop(1, nu)
    def _(d):
        for k in range(len(groups)):
            gather_u(d, k).wait_send()
        for h in range(PARTS):
            reduce_u(d, h).wait_send()
        spread_u(d).wait_send()

    @pl.when(jnp.logical_not(lead))
    def _():
        spread_u(0).wait_send()

    share_w.wait_send()

    @pl.loop(0, half)
    def _(j):
        @pl.when(jnp.logical_not(to_self(j)))
        def _():
            finish(j).wait_send()


def shards(sizes, text_query, vision_key, vision_value, grad_output, key_weight, value_weight):
    nu, ny, nk = sizes
    block = vision_key.shape[0]
    chunk = block * ny
    keys = chunk * nu
    tokens = text_query.shape[0]
    heads = text_query.shape[1] // HEAD
    rows = tokens * heads
    wide = key_weight.shape[0] * ny
    half = nu // 2
    vmem = pltpu.VMEM
    dma = pltpu.SemaphoreType.DMA
    return pl.pallas_call(
        lambda *refs: kernel(sizes, *refs),
        out_shape=(
            jax.ShapeDtypeStruct(text_query.shape, BF16),
            jax.ShapeDtypeStruct((block, wide), BF16),
        ),
        in_specs=[pl.BlockSpec(memory_space=pltpu.HBM)] * 6,
        out_specs=(pl.BlockSpec(memory_space=pltpu.VMEM),) * 2,
        scratch_shapes=[
            vmem((keys, 2 * HEAD), BF16),
            vmem((2, wide, 2 * HEAD), BF16),
            vmem((rows, HEAD), BF16),
            vmem((rows, HEAD), BF16),
            vmem((HEAD, rows), BF16),
            vmem((HEAD, rows), BF16),
            vmem((keys, rows), F32),
            vmem((keys, rows), F32),
            vmem((nu, 1, rows), F32),
            vmem((1, rows), F32),
            vmem((1, rows), F32),
            vmem((1, rows), F32),
            vmem((chunk // PARTS, rows), BF16),
            vmem((chunk // PARTS, rows), BF16),
            vmem((HEAD, rows), F32),
            vmem((nu, chunk, 2 * HEAD), BF16),
            vmem((nu, chunk, 2 * HEAD), BF16),
            vmem((chunk, 2 * HEAD), F32),
            vmem((ny, block, 2 * HEAD), BF16),
            vmem((ny, block, 2 * HEAD), BF16),
            vmem((block, 2 * HEAD), BF16),
            vmem((2, half, block, 2 * HEAD), BF16),
            vmem((half, block, wide), BF16),
            vmem((nk // 2, block, wide), BF16),
            vmem(text_query.shape, BF16),
            vmem(text_query.shape, BF16),
            dma((ny,)), dma((ny,)), dma((3, nu)), dma((3, nu)), dma((ny,)), dma((ny,)),
            dma((PARTS, nu)), dma((PARTS, nu)), dma((ny,)), dma((ny,)), dma((nu,)), dma((nu,)),
            dma((half,)), dma((nk // 2,)), dma((1,)), dma((1,)), dma((6,)),
        ],
        compiler_params=pltpu.CompilerParams(
            collective_id=0, has_side_effects=True, vmem_limit_bytes=60 * 1024 * 1024
        ),
    )(text_query, vision_key, vision_value, grad_output, key_weight, value_weight)


def solution(mesh):
    nk = mesh.shape["kv"]
    sizes = (nk, mesh.shape["seq"] // nk, nk)
    spec = P("seq", "kv")
    return jax.shard_map(
        lambda *arrays: shards(sizes, *arrays),
        mesh=mesh,
        in_specs=(spec,) * 6,
        out_specs=(spec, spec),
        check_vma=False,
    )
```

```python
import math

import jax
import jax.numpy as jnp
from jax import lax
from jax.experimental import pallas as pl
from jax.experimental.pallas import tpu as pltpu
from jax.sharding import PartitionSpec as P

HEAD = 128
SCALING = 1.0 / math.sqrt(HEAD)
EXP2_SCALE = SCALING * math.log2(math.e)
LANES = 256
PARTS = 2
STEP_IN = 1
STEP_OUT = 5
MESH = pl.DeviceIdType.MESH
F32 = jnp.float32
BF16 = jnp.bfloat16


def contract_last(a, b):
    return lax.dot_general(a, b, (((1,), (1,)), ((), ())), preferred_element_type=F32)


def kernel(
    sizes,
    query_ref, key_ref, value_ref, upstream_ref, key_weight_ref, value_weight_ref,
    grad_query_ref, grad_vision_ref,
    pairs, weights, query_rows, upstream_rows, query_t, upstream_t,
    exps, probs_grad, chunk_max, run_max, run_sum, run_dot,
    attn_low, logit_low, query_grad_t,
    term_send, term_recv, own_sum, row_send, row_recv, own_low, gathered,
    fin_send, fin_recv, query_in, upstream_in,
    gy_send, gy_recv, gu_send, gu_recv, wy_send, wy_recv,
    ru_send, ru_recv, ry_send, ry_recv, au_send, au_recv,
    fn_send, fn_recv, sb_send, sb_recv, in_sem,
):
    nu, ny, nk = sizes
    block = key_ref.shape[0]
    chunk = block * ny
    tokens = query_ref.shape[0]
    heads = query_ref.shape[1] // HEAD
    rows = tokens * heads
    wblock = key_weight_ref.shape[0]
    half = nu // 2
    s = lax.axis_index("seq")
    g = lax.axis_index("kv")
    u, y = s // ny, s % ny
    core, pair = g % 2, g // 2
    diag = jnp.where(u == g, 1, 0)

    def at(u_, y_, g_):
        return {"seq": u_ * ny + y_, "kv": g_}

    def u_peer(d):
        return at((u + d) % nu, y, g)

    def y_peer(d):
        return at(u, (y + d) % ny, g)

    def spread_to(d):
        return at((u + d) % nu, y, 2 * pair + u % 2)

    sibling = at(u, y, g + 1 - 2 * core)
    lead = core == u % 2

    def remote(src, dst, send, recv, device):
        return pltpu.make_async_remote_copy(
            src_ref=src, dst_ref=dst, send_sem=send, recv_sem=recv,
            device_id=device, device_id_type=MESH,
        )

    order = [0]
    for step in range(1, ny // 2 + 1):
        order += [r for r in (step, ny - step) if r not in order]
    groups = [(0, 1), (1, min(3, ny)), (min(3, ny), ny)]
    groups = [(lo, hi) for lo, hi in groups if hi > lo]

    def slots(lo, hi):
        return pl.ds(pl.multiple_of(u * chunk + lo * block, block), (hi - lo) * block)

    own_rows = slots(0, 1)
    own_w = pl.ds(pl.multiple_of(y * wblock, wblock), wblock)
    left, right = slice(0, HEAD), slice(HEAD, 2 * HEAD)
    loads = [
        pltpu.make_async_copy(src, dst, in_sem.at[i])
        for i, (src, dst) in enumerate((
            (key_ref, pairs.at[own_rows, left]),
            (value_ref, pairs.at[own_rows, right]),
            (query_ref, query_in),
            (upstream_ref, upstream_in),
            (key_weight_ref, weights.at[core, own_w, left]),
            (value_weight_ref, weights.at[core, own_w, right]),
        ))
    ]
    for load in loads:
        load.start()

    barrier = pltpu.get_barrier_semaphore()

    def greet(device):
        pl.semaphore_signal(barrier, inc=1, device_id=device, device_id_type=MESH)

    for d in range(1, ny):
        greet(y_peer(d))

    for d in range(1, nu):
        greet(u_peer(d))

    greet(sibling)

    @pl.loop(0, half)
    def _(k):
        @pl.when(2 * k + core != u)
        def _():
            greet(at(2 * k + core, y, g + 1 - 2 * core))

    @pl.loop(0, nk // 2)
    def _(j):
        source = 2 * j + u % 2

        @pl.when(jnp.logical_not((u == g) & (source == g)))
        def _():
            greet(at(g, y, source))

    loads[0].wait()
    loads[1].wait()
    pl.semaphore_wait(
        barrier, (ny - 1) + (nu - 1) + 1 + jnp.where(lead, 0, nu - 1) + half - diag
    )

    def gather_y(d):
        i = order.index(ny - d)
        return remote(
            pairs.at[own_rows], pairs.at[slots(i, i + 1)], gy_send.at[d], gy_recv.at[d], y_peer(d)
        )

    def gather_u(d, k):
        part = pairs.at[slots(*groups[k])]
        return remote(part, part, gu_send.at[k, d], gu_recv.at[k, d], u_peer(d))

    for i in reversed(range(1, ny)):
        gather_y(order[i]).start()

    for d in range(1, nu):
        gather_u(STEP_IN * d % nu, 0).start()

    loads[2].wait()
    loads[3].wait()
    for h in range(heads):
        at_cols = pl.ds(h * HEAD, HEAD)
        at_rows = pl.ds(h * tokens, tokens)
        q = query_in[:, at_cols]
        o = upstream_in[:, at_cols]
        query_rows[at_rows, :] = q
        upstream_rows[at_rows, :] = o
        query_t[:, at_rows] = q.T
        upstream_t[:, at_rows] = o.T
    run_max[...] = jnp.full_like(run_max, -1e30)
    run_sum[...] = jnp.zeros_like(run_sum)
    run_dot[...] = jnp.zeros_like(run_dot)
    query_grad_t[...] = jnp.zeros_like(query_grad_t)
    loads[4].wait()
    loads[5].wait()

    for k, (lo, hi) in enumerate(groups[1:], 1):
        for i in range(lo, hi):
            gather_y(ny - order[i]).wait_recv()

        for d in range(1, nu):
            gather_u(STEP_IN * d % nu, k).start()

    def gather_w(d):
        own = weights.at[core, own_w]
        return remote(own, own, wy_send.at[d], wy_recv.at[d], y_peer(d))

    @pl.loop(1, ny)
    def _(d):
        gather_w(d).start()

    @pl.loop(0, nu)
    def _(turn):
        d = STEP_IN * turn % nu

        @pl.when(turn > 0)
        def _():
            for k in range(len(groups)):
                gather_u(d, k).wait_recv()

        c = (u - d + nu) % nu
        at_c = pl.ds(pl.multiple_of(c * chunk, chunk), chunk)
        keys = pairs[at_c, :HEAD]
        values = pairs[at_c, HEAD:]
        for n in range(rows // LANES):
            cols = pl.ds(n * LANES, LANES)
            logits = jnp.dot(keys, query_t[:, cols], preferred_element_type=F32)
            gp = jnp.dot(values, upstream_t[:, cols], preferred_element_type=F32)
            old = run_max[:, cols]
            new = jnp.maximum(old, jnp.max(logits, axis=0, keepdims=True))
            factor = jnp.exp2((old - new) * EXP2_SCALE)
            e = jnp.exp2((logits - new) * EXP2_SCALE)
            run_max[:, cols] = new
            run_sum[:, cols] = run_sum[:, cols] * factor + jnp.sum(e, axis=0, keepdims=True)
            run_dot[:, cols] = run_dot[:, cols] * factor + jnp.sum(e * gp, axis=0, keepdims=True)
            exps[at_c, cols] = e
            probs_grad[at_c, cols] = gp
            chunk_max[c, :, cols] = new

    run_sum[...] = 1.0 / run_sum[...]
    run_dot[...] = run_dot[...] * run_sum[...]

    span = chunk // PARTS

    def reduce_u(d, h):
        rows_h = pl.ds(pl.multiple_of(h * span, span), span)
        return remote(
            term_send.at[d, rows_h], term_recv.at[d, rows_h],
            ru_send.at[h, d], ru_recv.at[h, d], u_peer(d),
        )

    @pl.loop(0, PARTS * nu)
    def _(t):
        h = PARTS - 1 - t // nu
        turn = 1 + t % nu
        d = jnp.where(turn == nu, nu, STEP_OUT * turn % nu)
        c = (u + d) % nu
        at_h = pl.ds(pl.multiple_of(h * span, span), span)
        at_c = pl.ds(pl.multiple_of(c * chunk + h * span, span), span)
        for n in range(rows // LANES):
            cols = pl.ds(n * LANES, LANES)
            share = (
                jnp.exp2((chunk_max[c, :, cols] - run_max[:, cols]) * EXP2_SCALE)
                * run_sum[:, cols]
            )
            a = exps[at_c, cols] * share
            attn_low[:, cols] = a.astype(BF16)
            logit_low[:, cols] = (
                a * (probs_grad[at_c, cols] - run_dot[:, cols]) * SCALING
            ).astype(BF16)
        key_term = jnp.dot(logit_low[...], query_rows[...], preferred_element_type=F32)
        value_term = jnp.dot(attn_low[...], upstream_rows[...], preferred_element_type=F32)

        @pl.when(d < nu)
        def _():
            term_send[d, at_h, left] = key_term.astype(BF16)
            term_send[d, at_h, right] = value_term.astype(BF16)
            reduce_u(d, h).start()

        @pl.when(d == nu)
        def _():
            own_sum[at_h, left] = key_term
            own_sum[at_h, right] = value_term

        keys_t = pairs[at_c, left].T
        query_grad_t[...] += jnp.dot(keys_t, logit_low[...], preferred_element_type=F32)

    for h in range(heads):
        grad_query_ref[:, pl.ds(h * HEAD, HEAD)] = (
            query_grad_t[:, pl.ds(h * tokens, tokens)].T.astype(BF16)
        )

    @pl.loop(1, ny)
    def _(d):
        gather_w(d).wait_recv()

    share_w = remote(
        weights.at[core], weights.at[core], sb_send.at[0], sb_recv.at[0], sibling
    )
    share_w.start()

    def reduce_y(d):
        return remote(row_send.at[d], row_recv.at[d], ry_send.at[d], ry_recv.at[d], y_peer(d))

    for h in reversed(range(PARTS)):
        at_h = pl.ds(h * span, span)

        @pl.loop(1, nu)
        def _(turn):
            d = STEP_OUT * turn % nu
            reduce_u(d, h).wait_recv()
            own_sum[at_h, :] += term_recv[d, at_h, :].astype(F32)

        for i in reversed(range(max(h * ny // PARTS, 1), (h + 1) * ny // PARTS)):
            row_send[order[i]] = own_sum[pl.ds(i * block, block), :].astype(BF16)
            reduce_y(order[i]).start()

    owned = own_sum[pl.ds(0, block), :]
    for i in range(1, ny):
        d = order[i]
        reduce_y(d).wait_recv()
        owned += row_recv[d].astype(F32)
    own_low[...] = owned.astype(BF16)

    def spread_u(d):
        return remote(
            own_low, gathered.at[core, u // 2], au_send.at[d], au_recv.at[core * half + u // 2], spread_to(d)
        )

    @pl.when(lead)
    def _():
        gathered[core, u // 2] = own_low[...]

    @pl.when(jnp.logical_not(lead))
    def _():
        spread_u(0).start()

    for d in range(1, nu):
        spread_u(d).start()

    share_w.wait_recv()

    @pl.loop(0, half)
    def _(k):
        for c in range(2):
            @pl.when(jnp.logical_not((2 * k + core == u) & (core == c)))
            def _():
                slot = gathered.at[c, k]
                remote(
                    slot, slot, au_send.at[0], au_recv.at[c * half + k], sibling
                ).wait_recv()

    for n in range(ny * wblock // LANES):
        cols = pl.ds(n * LANES, LANES)
        total = sum(
            contract_last(gathered[c].reshape(half * block, 2 * HEAD), weights[c, cols, :])
            for c in range(2)
        )
        fin_send[:, :, cols] = total.astype(BF16).reshape(half, block, LANES)

    def finish(j):
        return remote(
            fin_send.at[j], fin_recv.at[pair], fn_send.at[j], fn_recv.at[pair],
            at(2 * j + core, y, u),
        )

    def to_self(j):
        return (u == g) & (2 * j + core == u)

    @pl.loop(0, half)
    def _(j):
        @pl.when(jnp.logical_not(to_self(j)))
        def _():
            finish(j).start()

        @pl.when(to_self(j))
        def _():
            fin_recv[pair] = fin_send[j]

    @pl.loop(0, nk // 2)
    def _(j):
        @pl.when(jnp.logical_not((u == g) & (j == pair)))
        def _():
            remote(
                fin_send.at[0], fin_recv.at[j], fn_send.at[0], fn_recv.at[j], sibling
            ).wait_recv()

    result = fin_recv[0].astype(F32)
    for j in range(1, nk // 2):
        result += fin_recv[j].astype(F32)
    grad_vision_ref[...] = result.astype(BF16)

    for d in range(1, ny):
        gather_y(d).wait_send()
        gather_w(d).wait_send()
        reduce_y(d).wait_send()

    @pl.loop(1, nu)
    def _(d):
        for k in range(len(groups)):
            gather_u(d, k).wait_send()
        for h in range(PARTS):
            reduce_u(d, h).wait_send()
        spread_u(d).wait_send()

    @pl.when(jnp.logical_not(lead))
    def _():
        spread_u(0).wait_send()

    share_w.wait_send()

    @pl.loop(0, half)
    def _(j):
        @pl.when(jnp.logical_not(to_self(j)))
        def _():
            finish(j).wait_send()


def shards(sizes, text_query, vision_key, vision_value, grad_output, key_weight, value_weight):
    nu, ny, nk = sizes
    block = vision_key.shape[0]
    chunk = block * ny
    keys = chunk * nu
    tokens = text_query.shape[0]
    heads = text_query.shape[1] // HEAD
    rows = tokens * heads
    wide = key_weight.shape[0] * ny
    half = nu // 2
    vmem = pltpu.VMEM
    dma = pltpu.SemaphoreType.DMA
    return pl.pallas_call(
        lambda *refs: kernel(sizes, *refs),
        out_shape=(
            jax.ShapeDtypeStruct(text_query.shape, BF16),
            jax.ShapeDtypeStruct((block, wide), BF16),
        ),
        in_specs=[pl.BlockSpec(memory_space=pltpu.HBM)] * 6,
        out_specs=(pl.BlockSpec(memory_space=pltpu.VMEM),) * 2,
        scratch_shapes=[
            vmem((keys, 2 * HEAD), BF16),
            vmem((2, wide, 2 * HEAD), BF16),
            vmem((rows, HEAD), BF16),
            vmem((rows, HEAD), BF16),
            vmem((HEAD, rows), BF16),
            vmem((HEAD, rows), BF16),
            vmem((keys, rows), F32),
            vmem((keys, rows), F32),
            vmem((nu, 1, rows), F32),
            vmem((1, rows), F32),
            vmem((1, rows), F32),
            vmem((1, rows), F32),
            vmem((chunk // PARTS, rows), BF16),
            vmem((chunk // PARTS, rows), BF16),
            vmem((HEAD, rows), F32),
            vmem((nu, chunk, 2 * HEAD), BF16),
            vmem((nu, chunk, 2 * HEAD), BF16),
            vmem((chunk, 2 * HEAD), F32),
            vmem((ny, block, 2 * HEAD), BF16),
            vmem((ny, block, 2 * HEAD), BF16),
            vmem((block, 2 * HEAD), BF16),
            vmem((2, half, block, 2 * HEAD), BF16),
            vmem((half, block, wide), BF16),
            vmem((nk // 2, block, wide), BF16),
            vmem(text_query.shape, BF16),
            vmem(text_query.shape, BF16),
            dma((ny,)), dma((ny,)), dma((3, nu)), dma((3, nu)), dma((ny,)), dma((ny,)),
            dma((PARTS, nu)), dma((PARTS, nu)), dma((ny,)), dma((ny,)), dma((nu,)), dma((nu,)),
            dma((half,)), dma((nk // 2,)), dma((1,)), dma((1,)), dma((6,)),
        ],
        compiler_params=pltpu.CompilerParams(
            collective_id=0, has_side_effects=True, vmem_limit_bytes=60 * 1024 * 1024
        ),
    )(text_query, vision_key, vision_value, grad_output, key_weight, value_weight)


def solution(mesh):
    nk = mesh.shape["kv"]
    sizes = (nk, mesh.shape["seq"] // nk, nk)
    spec = P("seq", "kv")
    return jax.shard_map(
        lambda *arrays: shards(sizes, *arrays),
        mesh=mesh,
        in_specs=(spec,) * 6,
        out_specs=(spec, spec),
        check_vma=False,
    )
```

```python
import math

import jax
import jax.numpy as jnp
from jax import lax
from jax.experimental import pallas as pl
from jax.experimental.pallas import tpu as pltpu
from jax.sharding import PartitionSpec as P

HEAD = 128
SCALING = 1.0 / math.sqrt(HEAD)
EXP2_SCALE = SCALING * math.log2(math.e)
LANES = 256
PARTS = 2
STEP_IN = 5
STEP_OUT = 5
MESH = pl.DeviceIdType.MESH
F32 = jnp.float32
BF16 = jnp.bfloat16


def contract_last(a, b):
    return lax.dot_general(a, b, (((1,), (1,)), ((), ())), preferred_element_type=F32)


def kernel(
    sizes,
    query_ref, key_ref, value_ref, upstream_ref, key_weight_ref, value_weight_ref,
    grad_query_ref, grad_vision_ref,
    pairs, weights, query_rows, upstream_rows, query_t, upstream_t,
    exps, probs_grad, chunk_max, run_max, run_sum, run_dot,
    attn_low, logit_low, query_grad_t,
    term_send, term_recv, own_sum, row_send, row_recv, own_low, gathered,
    fin_send, fin_recv, query_in, upstream_in,
    gy_send, gy_recv, gu_send, gu_recv, wy_send, wy_recv,
    ru_send, ru_recv, ry_send, ry_recv, au_send, au_recv,
    fn_send, fn_recv, sb_send, sb_recv, in_sem,
):
    nu, ny, nk = sizes
    block = key_ref.shape[0]
    chunk = block * ny
    tokens = query_ref.shape[0]
    heads = query_ref.shape[1] // HEAD
    rows = tokens * heads
    wblock = key_weight_ref.shape[0]
    half = nu // 2
    s = lax.axis_index("seq")
    g = lax.axis_index("kv")
    u, y = s // ny, s % ny
    core, pair = g % 2, g // 2
    diag = jnp.where(u == g, 1, 0)

    def at(u_, y_, g_):
        return {"seq": u_ * ny + y_, "kv": g_}

    def u_peer(d):
        return at((u + d) % nu, y, g)

    def y_peer(d):
        return at(u, (y + d) % ny, g)

    def spread_to(d):
        return at((u + d) % nu, y, 2 * pair + u % 2)

    sibling = at(u, y, g + 1 - 2 * core)
    lead = core == u % 2

    def remote(src, dst, send, recv, device):
        return pltpu.make_async_remote_copy(
            src_ref=src, dst_ref=dst, send_sem=send, recv_sem=recv,
            device_id=device, device_id_type=MESH,
        )

    order = [0]
    for step in range(1, ny // 2 + 1):
        order += [r for r in (step, ny - step) if r not in order]
    groups = [(0, 1), (1, min(3, ny)), (min(3, ny), ny)]
    groups = [(lo, hi) for lo, hi in groups if hi > lo]

    def slots(lo, hi):
        return pl.ds(pl.multiple_of(u * chunk + lo * block, block), (hi - lo) * block)

    own_rows = slots(0, 1)
    own_w = pl.ds(pl.multiple_of(y * wblock, wblock), wblock)
    left, right = slice(0, HEAD), slice(HEAD, 2 * HEAD)
    loads = [
        pltpu.make_async_copy(src, dst, in_sem.at[i])
        for i, (src, dst) in enumerate((
            (key_ref, pairs.at[own_rows, left]),
            (value_ref, pairs.at[own_rows, right]),
            (query_ref, query_in),
            (upstream_ref, upstream_in),
            (key_weight_ref, weights.at[core, own_w, left]),
            (value_weight_ref, weights.at[core, own_w, right]),
        ))
    ]
    for load in loads:
        load.start()

    barrier = pltpu.get_barrier_semaphore()

    def greet(device):
        pl.semaphore_signal(barrier, inc=1, device_id=device, device_id_type=MESH)

    for d in range(1, ny):
        greet(y_peer(d))

    for d in range(1, nu):
        greet(u_peer(d))

    greet(sibling)

    @pl.loop(0, half)
    def _(k):
        @pl.when(2 * k + core != u)
        def _():
            greet(at(2 * k + core, y, g + 1 - 2 * core))

    @pl.loop(0, nk // 2)
    def _(j):
        source = 2 * j + u % 2

        @pl.when(jnp.logical_not((u == g) & (source == g)))
        def _():
            greet(at(g, y, source))

    loads[0].wait()
    loads[1].wait()
    pl.semaphore_wait(
        barrier, (ny - 1) + (nu - 1) + 1 + jnp.where(lead, 0, nu - 1) + half - diag
    )

    def gather_y(d):
        i = order.index(ny - d)
        return remote(
            pairs.at[own_rows], pairs.at[slots(i, i + 1)], gy_send.at[d], gy_recv.at[d], y_peer(d)
        )

    def gather_u(d, k):
        part = pairs.at[slots(*groups[k])]
        return remote(part, part, gu_send.at[k, d], gu_recv.at[k, d], u_peer(d))

    for i in reversed(range(1, ny)):
        gather_y(order[i]).start()

    for d in range(1, nu):
        gather_u(STEP_IN * d % nu, 0).start()

    loads[2].wait()
    loads[3].wait()
    for h in range(heads):
        at_cols = pl.ds(h * HEAD, HEAD)
        at_rows = pl.ds(h * tokens, tokens)
        q = query_in[:, at_cols]
        o = upstream_in[:, at_cols]
        query_rows[at_rows, :] = q
        upstream_rows[at_rows, :] = o
        query_t[:, at_rows] = q.T
        upstream_t[:, at_rows] = o.T
    run_max[...] = jnp.full_like(run_max, -1e30)
    run_sum[...] = jnp.zeros_like(run_sum)
    run_dot[...] = jnp.zeros_like(run_dot)
    query_grad_t[...] = jnp.zeros_like(query_grad_t)
    loads[4].wait()
    loads[5].wait()

    for k, (lo, hi) in enumerate(groups[1:], 1):
        for i in range(lo, hi):
            gather_y(ny - order[i]).wait_recv()

        for d in range(1, nu):
            gather_u(STEP_IN * d % nu, k).start()

    def gather_w(d):
        own = weights.at[core, own_w]
        return remote(own, own, wy_send.at[d], wy_recv.at[d], y_peer(d))

    @pl.loop(1, ny)
    def _(d):
        gather_w(d).start()

    @pl.loop(0, nu)
    def _(turn):
        d = STEP_IN * turn % nu

        @pl.when(turn > 0)
        def _():
            for k in range(len(groups)):
                gather_u(d, k).wait_recv()

        c = (u - d + nu) % nu
        at_c = pl.ds(pl.multiple_of(c * chunk, chunk), chunk)
        keys = pairs[at_c, :HEAD]
        values = pairs[at_c, HEAD:]
        for n in range(rows // LANES):
            cols = pl.ds(n * LANES, LANES)
            logits = jnp.dot(keys, query_t[:, cols], preferred_element_type=F32)
            gp = jnp.dot(values, upstream_t[:, cols], preferred_element_type=F32)
            old = run_max[:, cols]
            new = jnp.maximum(old, jnp.max(logits, axis=0, keepdims=True))
            factor = jnp.exp2((old - new) * EXP2_SCALE)
            e = jnp.exp2((logits - new) * EXP2_SCALE)
            run_max[:, cols] = new
            run_sum[:, cols] = run_sum[:, cols] * factor + jnp.sum(e, axis=0, keepdims=True)
            run_dot[:, cols] = run_dot[:, cols] * factor + jnp.sum(e * gp, axis=0, keepdims=True)
            exps[at_c, cols] = e
            probs_grad[at_c, cols] = gp
            chunk_max[c, :, cols] = new

    run_sum[...] = 1.0 / run_sum[...]
    run_dot[...] = run_dot[...] * run_sum[...]

    span = chunk // PARTS

    def reduce_u(d, h):
        rows_h = pl.ds(pl.multiple_of(h * span, span), span)
        return remote(
            term_send.at[d, rows_h], term_recv.at[d, rows_h],
            ru_send.at[h, d], ru_recv.at[h, d], u_peer(d),
        )

    @pl.loop(0, PARTS * nu)
    def _(t):
        h = PARTS - 1 - t // nu
        turn = 1 + t % nu
        d = jnp.where(turn == nu, nu, STEP_OUT * turn % nu)
        c = (u + d) % nu
        at_h = pl.ds(pl.multiple_of(h * span, span), span)
        at_c = pl.ds(pl.multiple_of(c * chunk + h * span, span), span)
        for n in range(rows // LANES):
            cols = pl.ds(n * LANES, LANES)
            share = (
                jnp.exp2((chunk_max[c, :, cols] - run_max[:, cols]) * EXP2_SCALE)
                * run_sum[:, cols]
            )
            a = exps[at_c, cols] * share
            attn_low[:, cols] = a.astype(BF16)
            logit_low[:, cols] = (
                a * (probs_grad[at_c, cols] - run_dot[:, cols]) * SCALING
            ).astype(BF16)
        key_term = jnp.dot(logit_low[...], query_rows[...], preferred_element_type=F32)
        value_term = jnp.dot(attn_low[...], upstream_rows[...], preferred_element_type=F32)

        @pl.when(d < nu)
        def _():
            term_send[d, at_h, left] = key_term.astype(BF16)
            term_send[d, at_h, right] = value_term.astype(BF16)
            reduce_u(d, h).start()

        @pl.when(d == nu)
        def _():
            own_sum[at_h, left] = key_term
            own_sum[at_h, right] = value_term

        keys_t = pairs[at_c, left].T
        query_grad_t[...] += jnp.dot(keys_t, logit_low[...], preferred_element_type=F32)

    for h in range(heads):
        grad_query_ref[:, pl.ds(h * HEAD, HEAD)] = (
            query_grad_t[:, pl.ds(h * tokens, tokens)].T.astype(BF16)
        )

    @pl.loop(1, ny)
    def _(d):
        gather_w(d).wait_recv()

    share_w = remote(
        weights.at[core], weights.at[core], sb_send.at[0], sb_recv.at[0], sibling
    )
    share_w.start()

    def reduce_y(d):
        return remote(row_send.at[d], row_recv.at[d], ry_send.at[d], ry_recv.at[d], y_peer(d))

    for h in reversed(range(PARTS)):
        at_h = pl.ds(h * span, span)

        @pl.loop(1, nu)
        def _(turn):
            d = STEP_OUT * turn % nu
            reduce_u(d, h).wait_recv()
            own_sum[at_h, :] += term_recv[d, at_h, :].astype(F32)

        for i in reversed(range(max(h * ny // PARTS, 1), (h + 1) * ny // PARTS)):
            row_send[order[i]] = own_sum[pl.ds(i * block, block), :].astype(BF16)
            reduce_y(order[i]).start()

    owned = own_sum[pl.ds(0, block), :]
    for i in range(1, ny):
        d = order[i]
        reduce_y(d).wait_recv()
        owned += row_recv[d].astype(F32)
    own_low[...] = owned.astype(BF16)

    def spread_u(d):
        return remote(
            own_low, gathered.at[core, u // 2], au_send.at[d], au_recv.at[core * half + u // 2], spread_to(d)
        )

    @pl.when(lead)
    def _():
        gathered[core, u // 2] = own_low[...]

    @pl.when(jnp.logical_not(lead))
    def _():
        spread_u(0).start()

    for d in range(1, nu):
        spread_u(d).start()

    share_w.wait_recv()

    @pl.loop(0, half)
    def _(k):
        for c in range(2):
            @pl.when(jnp.logical_not((2 * k + core == u) & (core == c)))
            def _():
                slot = gathered.at[c, k]
                remote(
                    slot, slot, au_send.at[0], au_recv.at[c * half + k], sibling
                ).wait_recv()

    for n in range(ny * wblock // LANES):
        cols = pl.ds(n * LANES, LANES)
        total = sum(
            contract_last(gathered[c].reshape(half * block, 2 * HEAD), weights[c, cols, :])
            for c in range(2)
        )
        fin_send[:, :, cols] = total.astype(BF16).reshape(half, block, LANES)

    def finish(j):
        return remote(
            fin_send.at[j], fin_recv.at[pair], fn_send.at[j], fn_recv.at[pair],
            at(2 * j + core, y, u),
        )

    def to_self(j):
        return (u == g) & (2 * j + core == u)

    @pl.loop(0, half)
    def _(j):
        @pl.when(jnp.logical_not(to_self(j)))
        def _():
            finish(j).start()

        @pl.when(to_self(j))
        def _():
            fin_recv[pair] = fin_send[j]

    @pl.loop(0, nk // 2)
    def _(j):
        @pl.when(jnp.logical_not((u == g) & (j == pair)))
        def _():
            remote(
                fin_send.at[0], fin_recv.at[j], fn_send.at[0], fn_recv.at[j], sibling
            ).wait_recv()

    result = fin_recv[0].astype(F32)
    for j in range(1, nk // 2):
        result += fin_recv[j].astype(F32)
    grad_vision_ref[...] = result.astype(BF16)

    for d in range(1, ny):
        gather_y(d).wait_send()
        gather_w(d).wait_send()
        reduce_y(d).wait_send()

    @pl.loop(1, nu)
    def _(d):
        for k in range(len(groups)):
            gather_u(d, k).wait_send()
        for h in range(PARTS):
            reduce_u(d, h).wait_send()
        spread_u(d).wait_send()

    @pl.when(jnp.logical_not(lead))
    def _():
        spread_u(0).wait_send()

    share_w.wait_send()

    @pl.loop(0, half)
    def _(j):
        @pl.when(jnp.logical_not(to_self(j)))
        def _():
            finish(j).wait_send()


def shards(sizes, text_query, vision_key, vision_value, grad_output, key_weight, value_weight):
    nu, ny, nk = sizes
    block = vision_key.shape[0]
    chunk = block * ny
    keys = chunk * nu
    tokens = text_query.shape[0]
    heads = text_query.shape[1] // HEAD
    rows = tokens * heads
    wide = key_weight.shape[0] * ny
    half = nu // 2
    vmem = pltpu.VMEM
    dma = pltpu.SemaphoreType.DMA
    return pl.pallas_call(
        lambda *refs: kernel(sizes, *refs),
        out_shape=(
            jax.ShapeDtypeStruct(text_query.shape, BF16),
            jax.ShapeDtypeStruct((block, wide), BF16),
        ),
        in_specs=[pl.BlockSpec(memory_space=pltpu.HBM)] * 6,
        out_specs=(pl.BlockSpec(memory_space=pltpu.VMEM),) * 2,
        scratch_shapes=[
            vmem((keys, 2 * HEAD), BF16),
            vmem((2, wide, 2 * HEAD), BF16),
            vmem((rows, HEAD), BF16),
            vmem((rows, HEAD), BF16),
            vmem((HEAD, rows), BF16),
            vmem((HEAD, rows), BF16),
            vmem((keys, rows), F32),
            vmem((keys, rows), F32),
            vmem((nu, 1, rows), F32),
            vmem((1, rows), F32),
            vmem((1, rows), F32),
            vmem((1, rows), F32),
            vmem((chunk // PARTS, rows), BF16),
            vmem((chunk // PARTS, rows), BF16),
            vmem((HEAD, rows), F32),
            vmem((nu, chunk, 2 * HEAD), BF16),
            vmem((nu, chunk, 2 * HEAD), BF16),
            vmem((chunk, 2 * HEAD), F32),
            vmem((ny, block, 2 * HEAD), BF16),
            vmem((ny, block, 2 * HEAD), BF16),
            vmem((block, 2 * HEAD), BF16),
            vmem((2, half, block, 2 * HEAD), BF16),
            vmem((half, block, wide), BF16),
            vmem((nk // 2, block, wide), BF16),
            vmem(text_query.shape, BF16),
            vmem(text_query.shape, BF16),
            dma((ny,)), dma((ny,)), dma((3, nu)), dma((3, nu)), dma((ny,)), dma((ny,)),
            dma((PARTS, nu)), dma((PARTS, nu)), dma((ny,)), dma((ny,)), dma((nu,)), dma((nu,)),
            dma((half,)), dma((nk // 2,)), dma((1,)), dma((1,)), dma((6,)),
        ],
        compiler_params=pltpu.CompilerParams(
            collective_id=0, has_side_effects=True, vmem_limit_bytes=60 * 1024 * 1024
        ),
    )(text_query, vision_key, vision_value, grad_output, key_weight, value_weight)


def solution(mesh):
    nk = mesh.shape["kv"]
    sizes = (nk, mesh.shape["seq"] // nk, nk)
    spec = P("seq", "kv")
    return jax.shard_map(
        lambda *arrays: shards(sizes, *arrays),
        mesh=mesh,
        in_specs=(spec,) * 6,
        out_specs=(spec, spec),
        check_vma=False,
    )
```
